32 devices in a mesh: fde: 8 (over z, x), pas: 4 (over y, core).
Axes of the slice: x: 2, y: 2, z: 4, core: 2. Of those that a mesh axis runs over, the one named last changes fastest.
Arguments:
- query_fixed_encoding: bfloat16 [128, 10240], P(None, 'fde'), may hold values from -6 to 6
- passage_fde: bfloat16 [1024, 10240], P('pas', 'fde'), may hold values from -0.0625 to 0.0625
- query_tokens: bfloat16 [128, 32, 128], P('fde'), may hold values from -6 to 6
- query_token_totals: int32 [128], P('fde'), may hold values from 1 to 32
- passage_tokens: bfloat16 [1024, 256, 128], P(('fde', 'pas')), may hold values from -0.5 to 0.5
- passage_lengths: int32 [1024], P(('fde', 'pas')), may hold values from 1 to 256
- candidates: int32 [128, 128], P('fde', 'pas'), may hold values from 0 to 1023, as said below
Outputs:
- fde_scores: float32 [128, 1024], P('fde', 'pas')
- rerank: float32 [128, 128], P('fde', 'pas')
The draws below stay inside these ranges and needn't reach their ends.
Inputs may be any that keep to these rules, and one draw needn't show every extreme that they name: Passage p is held by the device of linear index p // 32 over fde then pas. Among the 16 x 32 candidates held by one device, one quarter of the 32 devices (the same quarter for every device) is named exactly 48 times each, another quarter 2 times each, the rest not at all; within an owner device the ids are uniform and may repeat.
All inputs are finite; a program needn't handle non-finite values.
Results may differ from the reference program's by a relative error of at most 0.0003.
Values may be sent and summed in bfloat16 or wider, within the bound.
A program may use at most 128 MiB of HBM per device.

```python
import jax
import jax.numpy as jnp
import numpy as np
from jax import lax

Q_DEV = 16
C_DEV = 32
F = 10240
DIM = 128
QT = 32
PT = 256
PASS_DEV = 32
Q = 128
CAND = 128
OWNERS = 32
PASSAGES = 1024


def draw_candidates(key, part):
    quarter = OWNERS // 4
    mean_load = Q_DEV * C_DEV // OWNERS
    levels = np.concatenate([np.full(quarter, 3 * mean_load), np.full(quarter, mean_load), np.zeros(OWNERS - 2 * quarter)]).astype(np.int64)
    position = np.repeat(np.arange(OWNERS), levels).astype(np.int32)
    key_order, key_rest, key_local = jax.random.split(jax.random.fold_in(key, 17), 3)
    order = jax.random.permutation(key_order, jnp.arange(OWNERS, dtype=jnp.int32))
    hot_owners = order[:quarter]
    rare_passage_holders = order[quarter:]

    def one_source(source_key):
        key_cold, key_slots = jax.random.split(source_key)
        cold_mixed = jax.random.permutation(key_cold, rare_passage_holders)
        table = jnp.concatenate([hot_owners, cold_mixed])
        slot_order = jax.random.permutation(key_slots, jnp.asarray(position))
        return jnp.take(table, slot_order, axis=0)
    source_keys = jax.random.split(key_rest, OWNERS)
    owner_ids = jax.vmap(one_source)(source_keys)
    local_ids = jax.random.randint(key_local, (OWNERS, Q_DEV * C_DEV), 0, PASS_DEV, dtype=jnp.int32)
    passage_ids = owner_ids * PASS_DEV + local_ids
    groups = Q // Q_DEV
    shards = CAND // C_DEV
    arranged = passage_ids.reshape(groups, shards, Q_DEV, C_DEV)
    arranged = jnp.transpose(arranged, (0, 2, 1, 3)).reshape(Q, CAND)
    return arranged.astype(jnp.int32)


def with_ends(result, own_key, least, high):
    extent = result.shape
    index_at = [jax.random.randint(jax.random.fold_in(own_key, axis), (), 0, extent[axis]) for axis in range(len(extent))]
    result = result.at[tuple(index_at)].set(least)
    longest = extent.index(max(extent))
    index_at[longest] = (index_at[longest] + 1) % extent[longest]
    return result.at[tuple(index_at)].set(high)


def level_of(key, shape, cuts, least, top_value):
    def one(dim, parts):
        heights = jax.random.uniform(jax.random.fold_in(jax.random.fold_in(key, 6), dim), (parts,), jnp.float32, least / len(cuts), top_value / len(cuts))
        return jnp.repeat(jnp.exp(heights), shape[dim] // parts).reshape((-1,) + (1,) * (len(shape) - dim - 1))

    factor_of = one(*cuts[0])
    for cut in cuts[1:]:
        factor_of = factor_of * one(*cut)
    return factor_of


def bell_draw(own_key, shape, deviation, limit, pieces=(), held_as=jnp.bfloat16):
    drawn = deviation * jax.random.normal(own_key, shape, jnp.float32)
    if pieces:
        drawn = drawn * level_of(own_key, shape, pieces, -0.22, 0.18)
    return jnp.clip(drawn, -limit, limit).astype(held_as)


def setup_inputs(seed: int = 0) -> dict:
    splits = jax.random.split(jax.random.key(seed), 8)
    return {
        "query_fixed_encoding": bell_draw(splits[0], (Q, F), 1.0, 6.0, ((1, 8),)),
        "passage_fde": bell_draw(splits[1], (PASSAGES, F), F ** -0.5, 0.0625, ((0, 4), (1, 8))),
        "query_tokens": bell_draw(splits[2], (Q, QT, DIM), 1.0, 6.0, ((0, 8),)),
        "query_token_totals": with_ends(jax.random.randint(splits[3], (Q,), 1, QT + 1), jax.random.fold_in(splits[3], 1), 1, QT).astype(jnp.int32),
        "passage_tokens": bell_draw(splits[4], (PASSAGES, PT, DIM), DIM ** -0.5, 0.5, ((0, 32),)),
        "passage_lengths": with_ends(jax.random.randint(splits[5], (PASSAGES,), 1, PT + 1), jax.random.fold_in(splits[5], 1), 1, PT).astype(jnp.int32),
        "candidates": draw_candidates(jax.random.fold_in(splits[7], 71), 0),
    }


def reference(query_fixed_encoding, passage_fde, query_tokens, query_token_totals, passage_tokens, passage_lengths, candidates):
    query_wide = query_fixed_encoding.astype(jnp.float32)
    passage_blocks = passage_fde.reshape(OWNERS, PASS_DEV, F)

    def encode_block(block):
        return jnp.dot(query_wide, block.astype(jnp.float32).T, precision=lax.Precision.HIGHEST)

    block_scores = lax.map(encode_block, passage_blocks)
    fde_scores = jnp.transpose(block_scores, (1, 0, 2)).reshape(Q, PASSAGES)

    def per_query(inputs):
        token_vectors, count, passage_ids = inputs
        corpus_texts = jnp.take(passage_tokens, passage_ids, axis=0).astype(jnp.float32)
        lengths = jnp.take(passage_lengths, passage_ids, axis=0)
        similarity_matrix = jnp.einsum("jd,ctd->cjt", token_vectors.astype(jnp.float32), corpus_texts, precision=lax.Precision.HIGHEST)
        positions = jnp.arange(PT, dtype=jnp.int32)
        live = positions[None, None, :] < lengths[:, None, None]
        best_match = jnp.max(jnp.where(live, similarity_matrix, jnp.float32(-1e30)), axis=2)
        slots = jnp.arange(QT, dtype=jnp.int32)
        used = slots[None, :] < count
        summed = jnp.sum(jnp.where(used, best_match, jnp.float32(0.0)), axis=1)
        return summed / count.astype(jnp.float32)

    rerank = lax.map(per_query, (query_tokens, query_token_totals, candidates))
    return fde_scores, rerank
```

```python
import functools

import jax
import jax.numpy as jnp
from jax import lax
from jax.experimental import pallas as pl
from jax.experimental.pallas import tpu as pltpu
from jax.sharding import PartitionSpec as P

group = 8
chunk = 64
tile = 256


def maxsim_kernel(
    perm_ref, len_ref, level_ref, q_ref, seg_ref, p_ref, out_ref, packed, best
):
    pass_local, passage_slots, width = p_ref.shape
    levels_max = passage_slots // chunk
    rows = lax.broadcasted_iota(jnp.int32, (chunk, width), 0)

    def pack(i, carry):
        source = perm_ref[i]
        length = len_ref[i]
        head = p_ref[source, 0:1, :].astype(jnp.float32)
        for level in range(levels_max):
            block = p_ref[source, level * chunk : (level + 1) * chunk, :].astype(jnp.float32)
            block = jnp.where(rows + level * chunk < length, block, head)
            packed[i // group, level, i % group] = block.astype(jnp.bfloat16)
        return carry

    lax.fori_loop(0, pass_local, pack, 0)

    tiles = q_ref.shape[0] // tile
    out_ref[...] = jnp.zeros_like(out_ref)

    def one_tile(t, carry):
        vectors = q_ref[pl.ds(pl.multiple_of(t * tile, tile), tile), :]
        for g in range(pass_local // group):

            def step(level, acc):
                block = packed[g, level].reshape(group * chunk, width)
                similarity = lax.dot_general(
                    block, vectors, (((1,), (1,)), ((), ())), preferred_element_type=jnp.float32
                )
                similarity = similarity.reshape(group, chunk // 8, 8, tile)
                return jnp.maximum(acc, jnp.max(similarity, axis=1))

            acc = lax.fori_loop(
                0, level_ref[g], step, jnp.full((group, 8, tile), -3.0e38, jnp.float32)
            )
            found = jnp.max(acc, axis=1)
            for i in range(group):
                best[pl.ds(perm_ref[g * group + i], 1), :] = found[i : i + 1, :]
        queries = lax.broadcasted_iota(jnp.int32, (out_ref.shape[0], tile), 0)
        segment = seg_ref[pl.ds(t, 1), :]
        chosen = (queries == segment).astype(jnp.float32)
        out_ref[...] += lax.dot_general(
            chosen,
            best[...],
            (((1,), (1,)), ((), ())),
            preferred_element_type=jnp.float32,
            precision=lax.Precision.HIGHEST,
        )
        return carry

    lax.fori_loop(0, tiles, one_tile, 0)


def maxsim(tokens, segments, queries, passage_tokens, perm, lengths, levels):
    pass_local, passage_slots, width = passage_tokens.shape
    smem = pl.BlockSpec(memory_space=pltpu.SMEM)
    vmem = pl.BlockSpec(memory_space=pltpu.VMEM)
    return pl.pallas_call(
        maxsim_kernel,
        out_shape=jax.ShapeDtypeStruct((queries, pass_local), jnp.float32),
        in_specs=[smem, smem, smem, vmem, vmem, vmem],
        out_specs=vmem,
        scratch_shapes=[
            pltpu.VMEM((pass_local // group, passage_slots // chunk, group, chunk, width), jnp.bfloat16),
            pltpu.VMEM((pass_local, tile), jnp.float32),
        ],
        compiler_params=pltpu.CompilerParams(vmem_limit_bytes=40 * 1024 * 1024),
    )(perm, lengths, levels, tokens, segments, passage_tokens)


def body(
    query_fixed_encoding,
    passage_fde,
    query_tokens,
    query_token_totals,
    passage_tokens,
    passage_lengths,
    candidates,
):
    groups = lax.axis_size("fde")
    shards = lax.axis_size("pas")
    query_local, slots, width = query_tokens.shape
    pass_local = passage_tokens.shape[0]
    queries = groups * query_local

    live = lax.broadcasted_iota(jnp.int32, (query_local, slots, 1), 1) < query_token_totals[:, None, None]
    masked = jnp.where(live, query_tokens, jnp.bfloat16(0)).reshape(query_local * slots, width)
    tokens = lax.all_gather(masked, "fde", axis=0, tiled=True)

    incomplete = jnp.einsum(
        "qf,pf->qp", query_fixed_encoding, passage_fde, preferred_element_type=jnp.float32
    )
    fde_scores = lax.psum_scatter(incomplete, "fde", scatter_dimension=0, tiled=True)

    ids = jnp.arange(pass_local, dtype=jnp.int32)
    longer = (passage_lengths[None, :] > passage_lengths[:, None]) | (
        (passage_lengths[None, :] == passage_lengths[:, None]) & (ids[None, :] < ids[:, None])
    )
    rank = jnp.sum(longer.astype(jnp.int32), axis=1)
    placed = rank[None, :] == ids[:, None]
    perm = jnp.sum(jnp.where(placed, ids[None, :], 0), axis=1)
    lengths = jnp.sum(jnp.where(placed, passage_lengths[None, :], 0), axis=1)
    levels = (lengths[::group] + (chunk - 1)) // chunk
    segments = (jnp.arange(queries * slots, dtype=jnp.int32) // slots).reshape(-1, tile)

    table = maxsim(tokens, segments, queries, passage_tokens, perm, lengths, levels)
    back = lax.all_to_all(
        table.reshape(groups, query_local, pass_local), "fde", split_axis=0, concat_axis=0, tiled=True
    )
    back = lax.all_gather(back, "pas", axis=1)
    whole = jnp.transpose(back, (2, 0, 1, 3)).reshape(query_local, groups * shards * pass_local)
    every = jnp.arange(whole.shape[1], dtype=jnp.int32)
    rerank = jnp.sum(
        jnp.where(candidates[:, :, None] == every[None, None, :], whole[:, None, :], jnp.float32(0)), axis=2
    )
    rerank = rerank / query_token_totals.astype(jnp.float32)[:, None]
    return fde_scores, rerank


def solution(mesh):
    return jax.shard_map(
        body,
        mesh=mesh,
        in_specs=(
            P(None, "fde"),
            P("pas", "fde"),
            P("fde", None, None),
            P("fde"),
            P(("fde", "pas"), None, None),
            P(("fde", "pas")),
            P("fde", "pas"),
        ),
        out_specs=(P("fde", "pas"), P("fde", "pas")),
        check_vma=False,
    )
```

```python
import functools

import jax
import jax.numpy as jnp
from jax import lax
from jax.experimental import pallas as pl
from jax.experimental.pallas import tpu as pltpu
from jax.sharding import PartitionSpec as P

MESH = pl.DeviceIdType.MESH
group = 8
chunk = 64
tile = 2048
part_tile = 256
lanes = 128


def maxsim_kernel(perm_ref, len_ref, level_ref, q_ref, p_ref, out_ref, packed, acc_ref, best, table):
    pass_local, passage_slots, width = p_ref.shape
    slots = q_ref.shape[0] // table.shape[0]
    levels_max = passage_slots // chunk
    rows = lax.broadcasted_iota(jnp.int32, (chunk, width), 0)

    def pack(i, carry):
        source = perm_ref[i]
        length = len_ref[i]
        head = p_ref[source, 0:1, :].astype(jnp.float32)
        for level in range(levels_max):
            block = p_ref[source, level * chunk : (level + 1) * chunk, :].astype(jnp.float32)
            block = jnp.where(rows + level * chunk < length, block, head)
            packed[i // group, level, i % group] = block.astype(jnp.bfloat16)
        return carry

    lax.fori_loop(0, pass_local, pack, 0)
    per_tile = tile // slots
    chosen = (
        lax.broadcasted_iota(jnp.int32, (per_tile, tile), 0)
        == lax.broadcasted_iota(jnp.int32, (per_tile, tile), 1) // slots
    ).astype(jnp.float32)

    def one_tile(t, carry):
        start = pl.multiple_of(t * tile, tile)
        for g in range(pass_local // group):
            acc_ref[...] = jnp.full(acc_ref.shape, -3.0e38, jnp.float32)

            def step(level, carry):
                block = packed[g, level].reshape(group * chunk, width)
                for s in range(0, tile, part_tile):
                    vectors = q_ref[pl.ds(pl.multiple_of(start + s, part_tile), part_tile), :]
                    similarity = lax.dot_general(
                        block, vectors, (((1,), (1,)), ((), ())), preferred_element_type=jnp.float32
                    )
                    found = jnp.max(similarity.reshape(group, chunk // 8, 8, part_tile), axis=1)
                    acc_ref[:, :, s : s + part_tile] = jnp.maximum(
                        acc_ref[:, :, s : s + part_tile], found
                    )
                return carry

            lax.fori_loop(0, level_ref[g], step, 0)
            found = jnp.max(acc_ref[...], axis=1)
            for i in range(group):
                best[pl.ds(perm_ref[g * group + i], 1), :] = found[i : i + 1, :]
        table[pl.ds(pl.multiple_of(t * per_tile, per_tile), per_tile), :] = lax.dot_general(
            chosen,
            best[...],
            (((1,), (1,)), ((), ())),
            preferred_element_type=jnp.float32,
            precision=lax.Precision.HIGHEST,
        )
        return carry

    lax.fori_loop(0, q_ref.shape[0] // tile, one_tile, 0)
    groups = out_ref.shape[0]
    query_local = table.shape[0] // groups
    for g in range(groups):
        for c in range(query_local // 8):
            first = g * query_local + c * 8
            out_ref[g, :, c * pass_local : (c + 1) * pass_local] = table[first : first + 8, :]


def maxsim(tokens, groups, slots, passage_tokens, perm, lengths, levels):
    pass_local, passage_slots, width = passage_tokens.shape
    smem = pl.BlockSpec(memory_space=pltpu.SMEM)
    vmem = pl.BlockSpec(memory_space=pltpu.VMEM)
    return pl.pallas_call(
        maxsim_kernel,
        out_shape=jax.ShapeDtypeStruct((groups, 8, lanes), jnp.float32),
        in_specs=[smem, smem, smem, vmem, vmem],
        out_specs=vmem,
        scratch_shapes=[
            pltpu.VMEM((pass_local // group, passage_slots // chunk, group, chunk, width), jnp.bfloat16),
            pltpu.VMEM((group, 8, tile), jnp.float32),
            pltpu.VMEM((pass_local, tile), jnp.float32),
            pltpu.VMEM((tokens.shape[0] // slots, pass_local), jnp.float32),
        ],
        compiler_params=pltpu.CompilerParams(vmem_limit_bytes=40 * 1024 * 1024),
        name="maxsim",
    )(perm, lengths, levels, tokens, passage_tokens)


def axis_pair(here, there):
    return {"fde": here, "pas": there}


def gather_kernel(
    groups, shards, totals_ref, qfe_ref, pfde_ref, tok_ref, out_ref, fde_ref,
    part, landed, send_a, recv_a, send_b, recv_b, send_c, recv_c, send_s, recv_s,
):
    f = lax.axis_index("fde")
    p = lax.axis_index("pas")
    query_local, slots, width = tok_ref.shape
    half = shards // 2
    core = lax.rem(p, 2)
    other = p + 1 - 2 * core
    rows = query_local * slots // shards

    barrier = pltpu.get_barrier_semaphore()
    for d in range(1, groups):
        pl.semaphore_signal(barrier, inc=1, device_id=axis_pair(lax.rem(f + d, groups), p), device_id_type=MESH)
    for e in range(1, half):
        pl.semaphore_signal(barrier, inc=1, device_id=axis_pair(f, lax.rem(p + 2 * e, shards)), device_id_type=MESH)
    pl.semaphore_signal(barrier, inc=1, device_id=axis_pair(f, other), device_id_type=MESH)

    slot = lax.broadcasted_iota(jnp.int32, (slots, width), 0)
    for q in range(query_local):
        block = tok_ref[q].astype(jnp.float32)
        block = jnp.where(slot < totals_ref[q], block, jnp.float32(0))
        out_ref[f, q * slots : (q + 1) * slots, :] = block.astype(jnp.bfloat16)
    pl.semaphore_wait(barrier, groups - 1 + half)

    def piece(group, owner):
        place = lax.rem(owner, 2) * half + owner // 2
        return out_ref.at[group, pl.ds(pl.multiple_of(place * rows, rows), rows), :]

    first = []
    for d in range(1, groups):
        copy = pltpu.make_async_remote_copy(
            src_ref=piece(f, p), dst_ref=piece(f, p), send_sem=send_a.at[d], recv_sem=recv_a.at[d],
            device_id=axis_pair(lax.rem(f + d, groups), p), device_id_type=MESH,
        )
        copy.start()
        first.append(copy)

    for g in range(groups):
        q = qfe_ref[g * query_local : (g + 1) * query_local, :]
        part[g] = lax.dot_general(
            q, pfde_ref[...], (((1,), (1,)), ((), ())), preferred_element_type=jnp.float32
        )
    sums = []
    for d in range(1, groups):
        g = lax.rem(f + d, groups)
        copy = pltpu.make_async_remote_copy(
            src_ref=part.at[g], dst_ref=landed.at[d], send_sem=send_s.at[d], recv_sem=recv_s.at[d],
            device_id=axis_pair(g, p), device_id_type=MESH,
        )
        copy.start()
        sums.append(copy)

    second = []
    for d in range(1, groups):
        first[d - 1].wait_recv()
        g = lax.rem(f - d + groups, groups)
        for e in range(1, half):
            copy = pltpu.make_async_remote_copy(
                src_ref=piece(g, p), dst_ref=piece(g, p), send_sem=send_b.at[d, e], recv_sem=recv_b.at[d, e],
                device_id=axis_pair(f, lax.rem(p + 2 * e, shards)), device_id_type=MESH,
            )
            copy.start()
            second.append(copy)
    third = []
    for d in range(1, groups):
        g = lax.rem(f - d + groups, groups)
        for e in range(1, half):
            second[(d - 1) * (half - 1) + e - 1].wait_recv()
        mine = out_ref.at[g, pl.ds(pl.multiple_of(core * (half * rows), half * rows), half * rows), :]
        copy = pltpu.make_async_remote_copy(
            src_ref=mine, dst_ref=mine, send_sem=send_c.at[d], recv_sem=recv_c.at[d],
            device_id=axis_pair(f, other), device_id_type=MESH,
        )
        copy.start()
        third.append(copy)

    total = part[f]
    for d in range(1, groups):
        sums[d - 1].wait_recv()
        total = total + landed[d]
    fde_ref[...] = total
    for copy in third:
        copy.wait_recv()
    for copy in first + second + third + sums:
        copy.wait_send()


def gather(groups, shards, totals, query_fixed_encoding, passage_fde, query_tokens):
    query_local, slots, width = query_tokens.shape
    passages = passage_fde.shape[0]
    smem = pl.BlockSpec(memory_space=pltpu.SMEM)
    vmem = pl.BlockSpec(memory_space=pltpu.VMEM)
    half = shards // 2
    dma = pltpu.SemaphoreType.DMA
    return pl.pallas_call(
        functools.partial(gather_kernel, groups, shards),
        out_shape=(
            jax.ShapeDtypeStruct((groups, query_local * slots, width), jnp.bfloat16),
            jax.ShapeDtypeStruct((query_local, passages), jnp.float32),
        ),
        in_specs=[smem, vmem, vmem, vmem],
        out_specs=(vmem, vmem),
        scratch_shapes=[
            pltpu.VMEM((groups, query_local, passages), jnp.float32),
            pltpu.VMEM((groups, query_local, passages), jnp.float32),
            dma((groups,)), dma((groups,)),
            dma((groups, half)), dma((groups, half)),
            dma((groups,)), dma((groups,)),
            dma((groups,)), dma((groups,)),
        ],
        compiler_params=pltpu.CompilerParams(
            collective_id=0, has_side_effects=True, vmem_limit_bytes=40 * 1024 * 1024
        ),
        name="gather_tokens",
    )(totals, query_fixed_encoding, passage_fde, query_tokens)


def return_kernel(groups, shards, table_ref, out_ref, send_sem, recv_sem):
    f = lax.axis_index("fde")
    p = lax.axis_index("pas")
    me = f * shards + p
    owners = groups * shards
    barrier = pltpu.get_barrier_semaphore()

    def signal(d, carry):
        o = lax.rem(me + d, owners)
        pl.semaphore_signal(
            barrier, inc=1, device_id=axis_pair(o // shards, lax.rem(o, shards)), device_id_type=MESH
        )
        return carry

    lax.fori_loop(1, owners, signal, 0)
    out_ref[me] = table_ref[f]
    pl.semaphore_wait(barrier, owners - 1)

    def copy_to(d):
        o = lax.rem(me + d, owners)
        return pltpu.make_async_remote_copy(
            src_ref=table_ref.at[o // shards], dst_ref=out_ref.at[me],
            send_sem=send_sem.at[d], recv_sem=recv_sem.at[d],
            device_id=axis_pair(o // shards, lax.rem(o, shards)), device_id_type=MESH,
        )

    def start(d, carry):
        copy_to(d).start()
        return carry

    def finish(d, carry):
        copy_to(d).wait()
        return carry

    lax.fori_loop(1, owners, start, 0)
    lax.fori_loop(1, owners, finish, 0)


def send_back(groups, shards, table):
    owners = groups * shards
    vmem = pl.BlockSpec(memory_space=pltpu.VMEM)
    return pl.pallas_call(
        functools.partial(return_kernel, groups, shards),
        out_shape=jax.ShapeDtypeStruct((owners,) + table.shape[1:], table.dtype),
        in_specs=[vmem],
        out_specs=vmem,
        scratch_shapes=[pltpu.SemaphoreType.DMA((owners,)), pltpu.SemaphoreType.DMA((owners,))],
        compiler_params=pltpu.CompilerParams(collective_id=1, has_side_effects=True),
        name="send_back",
    )(table)


def body(
    query_fixed_encoding,
    passage_fde,
    query_tokens,
    query_token_totals,
    passage_tokens,
    passage_lengths,
    candidates,
):
    groups = lax.axis_size("fde")
    shards = lax.axis_size("pas")
    query_local, slots, width = query_tokens.shape
    pass_local = passage_tokens.shape[0]

    tokens, fde_scores = gather(
        groups, shards, query_token_totals, query_fixed_encoding, passage_fde, query_tokens
    )

    ids = jnp.arange(pass_local, dtype=jnp.int32)
    longer = (passage_lengths[None, :] > passage_lengths[:, None]) | (
        (passage_lengths[None, :] == passage_lengths[:, None]) & (ids[None, :] < ids[:, None])
    )
    rank = jnp.sum(longer.astype(jnp.int32), axis=1)
    placed = rank[None, :] == ids[:, None]
    perm = jnp.sum(jnp.where(placed, ids[None, :], 0), axis=1)
    lengths = jnp.sum(jnp.where(placed, passage_lengths[None, :], 0), axis=1)
    levels = (lengths[::group] + (chunk - 1)) // chunk

    table = maxsim(tokens.reshape(-1, width), groups, slots, passage_tokens, perm, lengths, levels)
    back = send_back(groups, shards, table)
    packs = query_local // 8
    whole = back[:, :, : packs * pass_local].reshape(groups * shards, 8, packs, pass_local)
    whole = jnp.transpose(whole, (2, 1, 0, 3)).reshape(query_local, groups * shards * pass_local)
    every = jnp.arange(whole.shape[1], dtype=jnp.int32)
    rerank = jnp.sum(
        jnp.where(candidates[:, :, None] == every[None, None, :], whole[:, None, :], jnp.float32(0)), axis=2
    )
    rerank = rerank / query_token_totals.astype(jnp.float32)[:, None]
    return fde_scores, rerank


def solution(mesh):
    return jax.shard_map(
        body,
        mesh=mesh,
        in_specs=(
            P(None, "fde"),
            P("pas", "fde"),
            P("fde", None, None),
            P("fde"),
            P(("fde", "pas"), None, None),
            P(("fde", "pas")),
            P("fde", "pas"),
        ),
        out_specs=(P("fde", "pas"), P("fde", "pas")),
        check_vma=False,
    )
```

```python
import functools

import jax
import jax.numpy as jnp
from jax import lax
from jax.experimental import pallas as pl
from jax.experimental.pallas import tpu as pltpu
from jax.sharding import PartitionSpec as P

MESH = pl.DeviceIdType.MESH
block = 16
part_tile = 256
lanes = 128


def axis_pair(here, there):
    return {"fde": here, "pas": there}


def kernel(
    groups, shards, totals_ref, len_ref, qfe_hbm, pfde_hbm, tok_hbm, pass_hbm, out_ref, fde_ref,
    qfe, pfde, own, packed, tokens, best, table, part, landed,
    load, send_a, recv_a, send_b, recv_b, send_c, recv_c, send_s, recv_s, send_r, recv_r,
):
    f = lax.axis_index("fde")
    p = lax.axis_index("pas")
    me = f * shards + p
    owners = groups * shards
    query_local, slots, width = own.shape
    pass_local, passage_slots, _ = packed.shape
    half = shards // 2
    core = lax.rem(p, 2)
    other = p + 1 - 2 * core
    rows = query_local * slots // shards

    loads = [
        pltpu.make_async_copy(source, target, load.at[i])
        for i, (source, target) in enumerate(
            ((tok_hbm, own), (pass_hbm, packed), (pfde_hbm, pfde), (qfe_hbm, qfe))
        )
    ]
    for copy in loads:
        copy.start()

    barrier = pltpu.get_barrier_semaphore()

    def signal(d, carry):
        o = lax.rem(me + d, owners)
        pl.semaphore_signal(
            barrier, inc=1, device_id=axis_pair(o // shards, lax.rem(o, shards)), device_id_type=MESH
        )
        return carry

    lax.fori_loop(1, owners, signal, 0)

    loads[0].wait()
    slot = lax.broadcasted_iota(jnp.int32, (slots, width), 0)
    for q in range(query_local):
        vectors = own[q].astype(jnp.float32)
        vectors = jnp.where(slot < totals_ref[q], vectors, jnp.float32(0))
        tokens[f, q * slots : (q + 1) * slots, :] = vectors.astype(jnp.bfloat16)

    loads[1].wait()
    place = lax.broadcasted_iota(jnp.int32, (passage_slots, width), 0)

    def fill(i, carry):
        first = packed[i, 0:1, :].astype(jnp.float32)
        whole = jnp.where(place < len_ref[i], packed[i].astype(jnp.float32), first)
        packed[i] = whole.astype(jnp.bfloat16)
        return carry

    lax.fori_loop(0, pass_local, fill, 0)
    table[...] = jnp.zeros_like(table)
    pl.semaphore_wait(barrier, owners - 1)

    def piece(g, owner):
        at = lax.rem(owner, 2) * half + owner // 2
        return tokens.at[g, pl.ds(pl.multiple_of(at * rows, rows), rows), :]

    first = []
    for d in range(1, groups):
        copy = pltpu.make_async_remote_copy(
            src_ref=piece(f, p), dst_ref=piece(f, p), send_sem=send_a.at[d], recv_sem=recv_a.at[d],
            device_id=axis_pair(lax.rem(f + d, groups), p), device_id_type=MESH,
        )
        copy.start()
        first.append(copy)

    columns = query_local * slots
    chosen = (
        lax.broadcasted_iota(jnp.int32, (query_local, columns), 0)
        == lax.broadcasted_iota(jnp.int32, (query_local, columns), 1) // slots
    ).astype(jnp.float32)

    def score(g, d):
        def step(i, carry):
            passages = packed[pl.ds(i * block, block)].reshape(block * passage_slots, width)
            for s in range(0, columns, part_tile):
                similarity = lax.dot_general(
                    passages,
                    tokens[g, s : s + part_tile, :],
                    (((1,), (1,)), ((), ())),
                    preferred_element_type=jnp.float32,
                )
                found = jnp.max(similarity.reshape(block, passage_slots // 8, 8, part_tile), axis=1)
                best[i, :, s : s + part_tile] = jnp.max(found, axis=1)
            return carry

        lax.fori_loop(0, pass_local // block, step, 0)
        summed = lax.dot_general(
            chosen,
            best[...].reshape(pass_local, columns),
            (((1,), (1,)), ((), ())),
            preferred_element_type=jnp.float32,
            precision=lax.Precision.HIGHEST,
        )
        for c in range(query_local // 8):
            table[d, :, c * pass_local : (c + 1) * pass_local] = summed[c * 8 : (c + 1) * 8, :]

    def home(d, e):
        at = d * shards + e
        return pltpu.make_async_remote_copy(
            src_ref=table.at[d], dst_ref=out_ref.at[me],
            send_sem=send_r.at[at], recv_sem=recv_r.at[at],
            device_id=axis_pair(lax.rem(f - d + groups, groups), lax.rem(p + e, shards)),
            device_id_type=MESH,
        )

    def send_home(d, least):
        def go(e, carry):
            home(d, e).start()
            return carry

        lax.fori_loop(least, shards, go, 0)

    score(f, 0)
    out_ref[me] = table[0]
    send_home(0, 1)

    second = []
    for d in range(1, groups):
        first[d - 1].wait_recv()
        g = lax.rem(f - d + groups, groups)
        for e in range(1, half):
            copy = pltpu.make_async_remote_copy(
                src_ref=piece(g, p), dst_ref=piece(g, p), send_sem=send_b.at[d, e], recv_sem=recv_b.at[d, e],
                device_id=axis_pair(f, lax.rem(p + 2 * e, shards)), device_id_type=MESH,
            )
            copy.start()
            second.append(copy)

    loads[2].wait()
    loads[3].wait()
    for g in range(groups):
        part[g] = lax.dot_general(
            qfe[g * query_local : (g + 1) * query_local, :],
            pfde[...],
            (((1,), (1,)), ((), ())),
            preferred_element_type=jnp.float32,
        )

    third = []
    for d in range(1, groups):
        g = lax.rem(f - d + groups, groups)
        for e in range(1, half):
            second[(d - 1) * (half - 1) + e - 1].wait_recv()
        mine = tokens.at[g, pl.ds(pl.multiple_of(core * (half * rows), half * rows), half * rows), :]
        copy = pltpu.make_async_remote_copy(
            src_ref=mine, dst_ref=mine, send_sem=send_c.at[d], recv_sem=recv_c.at[d],
            device_id=axis_pair(f, other), device_id_type=MESH,
        )
        copy.start()
        third.append(copy)

    sums = []
    for d in range(1, groups):
        g = lax.rem(f + d, groups)
        copy = pltpu.make_async_remote_copy(
            src_ref=part.at[g], dst_ref=landed.at[d], send_sem=send_s.at[d], recv_sem=recv_s.at[d],
            device_id=axis_pair(g, p), device_id_type=MESH,
        )
        copy.start()
        sums.append(copy)

    def one_group(d, carry):
        g = lax.rem(f - d + groups, groups)
        mine = tokens.at[g, pl.ds(pl.multiple_of(core * (half * rows), half * rows), half * rows), :]
        pltpu.make_async_remote_copy(
            src_ref=mine, dst_ref=mine, send_sem=send_c.at[d], recv_sem=recv_c.at[d],
            device_id=axis_pair(f, other), device_id_type=MESH,
        ).wait_recv()
        score(g, d)
        send_home(d, 0)
        return carry

    lax.fori_loop(1, groups, one_group, 0)

    total = part[f]
    for d in range(1, groups):
        sums[d - 1].wait_recv()
        total = total + landed[d]
    fde_ref[...] = total
    for copy in first + second + third + sums:
        copy.wait_send()

    def finish(at, carry):
        home(at // shards, lax.rem(at, shards)).wait()
        return carry

    lax.fori_loop(1, owners, finish, 0)


def call(groups, shards, totals, lengths, qfe, pfde, query_tokens, passage_tokens):
    query_local, slots, width = query_tokens.shape
    pass_local, passage_slots, _ = passage_tokens.shape
    passages = pfde.shape[0]
    owners = groups * shards
    half = shards // 2
    smem = pl.BlockSpec(memory_space=pltpu.SMEM)
    vmem = pl.BlockSpec(memory_space=pltpu.VMEM)
    far = pl.BlockSpec(memory_space=pl.ANY)
    dma = pltpu.SemaphoreType.DMA
    bf16, f32 = jnp.bfloat16, jnp.float32
    columns = query_local * slots
    return pl.pallas_call(
        functools.partial(kernel, groups, shards),
        out_shape=(
            jax.ShapeDtypeStruct((owners, 8, lanes), f32),
            jax.ShapeDtypeStruct((query_local, passages), f32),
        ),
        in_specs=[smem, smem, far, far, far, far],
        out_specs=(vmem, vmem),
        scratch_shapes=[
            pltpu.VMEM(qfe.shape, bf16),
            pltpu.VMEM(pfde.shape, bf16),
            pltpu.VMEM(query_tokens.shape, bf16),
            pltpu.VMEM(passage_tokens.shape, bf16),
            pltpu.VMEM((groups, columns, width), bf16),
            pltpu.VMEM((pass_local // block, block, columns), f32),
            pltpu.VMEM((groups, 8, lanes), f32),
            pltpu.VMEM((groups, query_local, passages), f32),
            pltpu.VMEM((groups, query_local, passages), f32),
            dma((4,)),
            dma((groups,)), dma((groups,)),
            dma((groups, half)), dma((groups, half)),
            dma((groups,)), dma((groups,)),
            dma((groups,)), dma((groups,)),
            dma((owners,)), dma((owners,)),
        ],
        compiler_params=pltpu.CompilerParams(
            collective_id=0, has_side_effects=True, vmem_limit_bytes=40 * 1024 * 1024
        ),
        name="retrieve",
    )(totals, lengths, qfe, pfde, query_tokens, passage_tokens)


def body(
    query_fixed_encoding,
    passage_fde,
    query_tokens,
    query_token_totals,
    passage_tokens,
    passage_lengths,
    candidates,
):
    groups = lax.axis_size("fde")
    shards = lax.axis_size("pas")
    query_local, slots, width = query_tokens.shape
    pass_local = passage_tokens.shape[0]

    back, fde_scores = call(
        groups, shards, query_token_totals, passage_lengths,
        query_fixed_encoding, passage_fde, query_tokens, passage_tokens,
    )
    packs = query_local // 8
    whole = back[:, :, : packs * pass_local].reshape(groups * shards, 8, packs, pass_local)
    whole = jnp.transpose(whole, (2, 1, 0, 3)).reshape(query_local, groups * shards * pass_local)
    every = jnp.arange(whole.shape[1], dtype=jnp.int32)
    rerank = jnp.sum(
        jnp.where(candidates[:, :, None] == every[None, None, :], whole[:, None, :], jnp.float32(0)), axis=2
    )
    rerank = rerank / query_token_totals.astype(jnp.float32)[:, None]
    return fde_scores, rerank


def solution(mesh):
    return jax.shard_map(
        body,
        mesh=mesh,
        in_specs=(
            P(None, "fde"),
            P("pas", "fde"),
            P("fde", None, None),
            P("fde"),
            P(("fde", "pas"), None, None),
            P(("fde", "pas")),
            P("fde", "pas"),
        ),
        out_specs=(P("fde", "pas"), P("fde", "pas")),
        check_vma=False,
    )
```

```python
import functools

import jax
import jax.numpy as jnp
from jax import lax
from jax.experimental import pallas as pl
from jax.experimental.pallas import tpu as pltpu
from jax.sharding import PartitionSpec as P

MESH = pl.DeviceIdType.MESH
block = 16
part_tile = 256
lanes = 128


def axis_pair(here, there):
    return {"fde": here, "pas": there}


def kernel(
    groups, shards, totals_ref, len_ref, qfe_hbm, pfde_hbm, tok_hbm, pass_hbm, out_ref, fde_ref,
    qfe, pfde, own, packed, tokens, best, table, part, landed,
    load, send_a, recv_a, send_b, recv_b, send_c, recv_c, send_s, recv_s, send_r, recv_r,
):
    f = lax.axis_index("fde")
    p = lax.axis_index("pas")
    me = f * shards + p
    owners = groups * shards
    query_local, slots, width = own.shape
    pass_local, passage_slots, _ = packed.shape
    half = shards // 2
    core = lax.rem(p, 2)
    other = p + 1 - 2 * core
    rows = query_local * slots // shards

    loads = [
        pltpu.make_async_copy(source, target, load.at[i])
        for i, (source, target) in enumerate(
            ((tok_hbm, own), (pass_hbm, packed), (pfde_hbm, pfde), (qfe_hbm, qfe))
        )
    ]
    for copy in loads:
        copy.start()

    barrier = pltpu.get_barrier_semaphore()

    def signal(d, carry):
        o = lax.rem(me + d, owners)
        pl.semaphore_signal(
            barrier, inc=1, device_id=axis_pair(o // shards, lax.rem(o, shards)), device_id_type=MESH
        )
        return carry

    lax.fori_loop(1, owners, signal, 0)

    loads[0].wait()
    slot = lax.broadcasted_iota(jnp.int32, (slots, width), 0)
    for q in range(query_local):
        vectors = own[q].astype(jnp.float32)
        vectors = jnp.where(slot < totals_ref[q], vectors, jnp.float32(0))
        tokens[f, q * slots : (q + 1) * slots, :] = vectors.astype(jnp.bfloat16)

    table[...] = jnp.zeros_like(table)
    pl.semaphore_wait(barrier, owners - 1)

    def piece(g, owner):
        at = lax.rem(owner, 2) * half + owner // 2
        return tokens.at[g, pl.ds(pl.multiple_of(at * rows, rows), rows), :]

    def halves(g):
        return tokens.at[g, pl.ds(pl.multiple_of(core * (half * rows), half * rows), half * rows), :]

    def spread(d):
        return pltpu.make_async_remote_copy(
            src_ref=piece(f, p), dst_ref=piece(f, p), send_sem=send_a.at[d], recv_sem=recv_a.at[d],
            device_id=axis_pair(lax.rem(f + d, groups), p), device_id_type=MESH,
        )

    def across(d, e):
        g = lax.rem(f - d + groups, groups)
        return pltpu.make_async_remote_copy(
            src_ref=piece(g, p), dst_ref=piece(g, p), send_sem=send_b.at[d, e], recv_sem=recv_b.at[d, e],
            device_id=axis_pair(f, lax.rem(p + 2 * e, shards)), device_id_type=MESH,
        )

    def to_core(d):
        g = lax.rem(f - d + groups, groups)
        return pltpu.make_async_remote_copy(
            src_ref=halves(g), dst_ref=halves(g), send_sem=send_c.at[d], recv_sem=recv_c.at[d],
            device_id=axis_pair(f, other), device_id_type=MESH,
        )

    def pass_across(d):
        spread(d).wait_recv()
        for e in range(1, half):
            across(d, e).start()

    def pass_to_core(d):
        for e in range(1, half):
            across(d, e).wait_recv()
        to_core(d).start()

    for d in range(1, groups):
        spread(d).start()

    loads[1].wait()
    place = lax.broadcasted_iota(jnp.int32, (passage_slots, width), 0)

    def fill(i, carry):
        first = packed[i, 0:1, :].astype(jnp.float32)
        whole = jnp.where(place < len_ref[i], packed[i].astype(jnp.float32), first)
        packed[i] = whole.astype(jnp.bfloat16)
        return carry

    lax.fori_loop(0, pass_local, fill, 0)

    columns = query_local * slots
    chosen = (
        lax.broadcasted_iota(jnp.int32, (query_local, columns), 0)
        == lax.broadcasted_iota(jnp.int32, (query_local, columns), 1) // slots
    ).astype(jnp.float32)

    def score_block(g, i):
        passages = packed[pl.ds(i * block, block)].reshape(block * passage_slots, width)
        for s in range(0, columns, part_tile):
            similarity = lax.dot_general(
                passages,
                tokens[g, s : s + part_tile, :],
                (((1,), (1,)), ((), ())),
                preferred_element_type=jnp.float32,
            )
            found = jnp.max(similarity.reshape(block, passage_slots // 8, 8, part_tile), axis=1)
            best[i, :, s : s + part_tile] = jnp.max(found, axis=1)

    def total_up(d):
        summed = lax.dot_general(
            chosen,
            best[...].reshape(pass_local, columns),
            (((1,), (1,)), ((), ())),
            preferred_element_type=jnp.float32,
            precision=lax.Precision.HIGHEST,
        )
        for c in range(query_local // 8):
            table[d, :, c * pass_local : (c + 1) * pass_local] = summed[c * 8 : (c + 1) * 8, :]

    def home(d, e):
        at = d * shards + e
        return pltpu.make_async_remote_copy(
            src_ref=table.at[d], dst_ref=out_ref.at[me],
            send_sem=send_r.at[at], recv_sem=recv_r.at[at],
            device_id=axis_pair(lax.rem(f - d + groups, groups), lax.rem(p + e, shards)),
            device_id_type=MESH,
        )

    def send_home(d, least):
        def go(e, carry):
            home(d, e).start()
            return carry

        lax.fori_loop(least, shards, go, 0)

    loads[2].wait()
    loads[3].wait()
    for g in range(groups):
        part[g] = lax.dot_general(
            qfe[g * query_local : (g + 1) * query_local, :],
            pfde[...],
            (((1,), (1,)), ((), ())),
            preferred_element_type=jnp.float32,
        )

    blocks = pass_local // block
    for d in range(1, min(3, groups)):
        pass_across(d)
    for i in range(blocks - 1):
        score_block(f, i)
    for d in range(3, min(4, groups)):
        pass_across(d)
    pass_to_core(1)
    score_block(f, blocks - 1)
    total_up(0)
    out_ref[me] = table[0]
    send_home(0, 1)

    sums = []
    for d in range(1, groups):
        g = lax.rem(f + d, groups)
        copy = pltpu.make_async_remote_copy(
            src_ref=part.at[g], dst_ref=landed.at[d], send_sem=send_s.at[d], recv_sem=recv_s.at[d],
            device_id=axis_pair(g, p), device_id_type=MESH,
        )
        copy.start()
        sums.append(copy)

    def one_group(d, carry):
        g = lax.rem(f - d + groups, groups)

        @pl.when(d + 3 < groups)
        def _():
            pass_across(d + 3)

        @pl.when(d + 1 < groups)
        def _():
            pass_to_core(d + 1)

        to_core(d).wait_recv()
        for i in range(blocks):
            score_block(g, i)
        total_up(d)
        send_home(d, 0)
        return carry

    lax.fori_loop(1, groups, one_group, 0)

    total = part[f]
    for d in range(1, groups):
        sums[d - 1].wait_recv()
        total = total + landed[d]
    fde_ref[...] = total
    for copy in sums:
        copy.wait_send()
    for d in range(1, groups):
        spread(d).wait_send()
        for e in range(1, half):
            across(d, e).wait_send()
        to_core(d).wait_send()

    def finish(at, carry):
        home(at // shards, lax.rem(at, shards)).wait()
        return carry

    lax.fori_loop(1, owners, finish, 0)


def call(groups, shards, totals, lengths, qfe, pfde, query_tokens, passage_tokens):
    query_local, slots, width = query_tokens.shape
    pass_local, passage_slots, _ = passage_tokens.shape
    passages = pfde.shape[0]
    owners = groups * shards
    half = shards // 2
    smem = pl.BlockSpec(memory_space=pltpu.SMEM)
    vmem = pl.BlockSpec(memory_space=pltpu.VMEM)
    far = pl.BlockSpec(memory_space=pl.ANY)
    dma = pltpu.SemaphoreType.DMA
    bf16, f32 = jnp.bfloat16, jnp.float32
    columns = query_local * slots
    return pl.pallas_call(
        functools.partial(kernel, groups, shards),
        out_shape=(
            jax.ShapeDtypeStruct((owners, 8, lanes), f32),
            jax.ShapeDtypeStruct((query_local, passages), f32),
        ),
        in_specs=[smem, smem, far, far, far, far],
        out_specs=(vmem, vmem),
        scratch_shapes=[
            pltpu.VMEM(qfe.shape, bf16),
            pltpu.VMEM(pfde.shape, bf16),
            pltpu.VMEM(query_tokens.shape, bf16),
            pltpu.VMEM(passage_tokens.shape, bf16),
            pltpu.VMEM((groups, columns, width), bf16),
            pltpu.VMEM((pass_local // block, block, columns), f32),
            pltpu.VMEM((groups, 8, lanes), f32),
            pltpu.VMEM((groups, query_local, passages), f32),
            pltpu.VMEM((groups, query_local, passages), f32),
            dma((4,)),
            dma((groups,)), dma((groups,)),
            dma((groups, half)), dma((groups, half)),
            dma((groups,)), dma((groups,)),
            dma((groups,)), dma((groups,)),
            dma((owners,)), dma((owners,)),
        ],
        compiler_params=pltpu.CompilerParams(
            collective_id=0, has_side_effects=True, vmem_limit_bytes=60 * 1024 * 1024
        ),
        name="retrieve",
    )(totals, lengths, qfe, pfde, query_tokens, passage_tokens)


def body(
    query_fixed_encoding,
    passage_fde,
    query_tokens,
    query_token_totals,
    passage_tokens,
    passage_lengths,
    candidates,
):
    groups = lax.axis_size("fde")
    shards = lax.axis_size("pas")
    query_local, slots, width = query_tokens.shape
    pass_local = passage_tokens.shape[0]

    back, fde_scores = call(
        groups, shards, query_token_totals, passage_lengths,
        query_fixed_encoding, passage_fde, query_tokens, passage_tokens,
    )
    packs = query_local // 8
    whole = back[:, :, : packs * pass_local].reshape(groups * shards, 8, packs, pass_local)
    whole = jnp.transpose(whole, (2, 1, 0, 3)).reshape(query_local, groups * shards * pass_local)
    every = jnp.arange(whole.shape[1], dtype=jnp.int32)
    rerank = jnp.sum(
        jnp.where(candidates[:, :, None] == every[None, None, :], whole[:, None, :], jnp.float32(0)), axis=2
    )
    rerank = rerank / query_token_totals.astype(jnp.float32)[:, None]
    return fde_scores, rerank


def solution(mesh):
    return jax.shard_map(
        body,
        mesh=mesh,
        in_specs=(
            P(None, "fde"),
            P("pas", "fde"),
            P("fde", None, None),
            P("fde"),
            P(("fde", "pas"), None, None),
            P(("fde", "pas")),
            P("fde", "pas"),
        ),
        out_specs=(P("fde", "pas"), P("fde", "pas")),
        check_vma=False,
    )
```
